32 devices in a mesh: wide: 4 (over y, x), narrow: 8 (over z, core).
Axes of the slice: x: 2, y: 2, z: 4, core: 2. Of those that a mesh axis runs over, the one named last changes fastest.
Arguments:
- tensor3: bfloat16 [256, 512, 512], P('wide', 'narrow'), may hold values from -6 to 6
- pattern: int32 [4, 8, 8], P('wide', 'narrow'), may hold values 0 or 1
- orbitals: bfloat16 [512, 256], P('narrow'), may hold values from -0.015625 to 0.015625
- metric: bfloat16 [256, 256], replicated, may hold values from -1 to 2, as said below
Outputs:
- exchange_matrix: float32 [512, 512], P(('wide', 'narrow'))
The draws below stay inside these ranges and needn't reach their ends.
Inputs may be any that keep to these rules, and one draw needn't show every extreme that they name: metric is symmetric.
All inputs are finite; a program needn't handle non-finite values. No bound on the sum of `pattern` on one device may be relied on, other than what follows from the above.
Results may differ from the reference program's by a relative error of at most 0.0006.
Values may be sent and summed in bfloat16 or wider, within the bound.
A program may use at most 128 MiB of HBM per device.

```python
import math
import jax
import jax.numpy as jnp
from jax import lax

BLK = 64
OCC = 256
RI = 256
NU = 512


def draw_metric(key, part):
    entries = jnp.clip(jax.random.normal(key, (RI, RI), jnp.float32), -4.0, 4.0)
    coupling = (entries + entries.T) * (0.5 / math.sqrt(RI))
    identity = (lax.broadcasted_iota(jnp.int32, (RI, RI), 0) == lax.broadcasted_iota(jnp.int32, (RI, RI), 1)).astype(jnp.float32)
    return (coupling + identity).astype(jnp.bfloat16)


def place_ends(array, key, smallest, high):
    place = [jax.random.randint(jax.random.fold_in(key, axis), (), 0, length) for axis, length in enumerate(array.shape)]
    longest = array.shape.index(max(array.shape))
    next_to = place[:longest] + [(place[longest] + 1) % array.shape[longest]] + place[longest + 1:]
    return array.at[tuple(place)].set(smallest).at[tuple(next_to)].set(high)


def steps_of(key, extent, cuts, smallest, top_value):
    def one(position, parts):
        draws = jax.random.uniform(jax.random.fold_in(jax.random.fold_in(key, 6), position), (parts,), jnp.float32, smallest / len(cuts), top_value / len(cuts))
        return jnp.repeat(jnp.exp(draws), extent[position] // parts).reshape((-1,) + (1,) * (len(extent) - position - 1))

    loudness = one(*cuts[0])
    for cut in cuts[1:]:
        loudness = loudness * one(*cut)
    return loudness


def normal_values(key, dims, spread, most, shards=(), held_as=jnp.bfloat16):
    values = jax.random.normal(key, dims, jnp.float32) * spread
    if len(shards) > 0:
        values = steps_of(key, dims, shards, -0.22, 0.18) * values
    return jnp.clip(values, min=-most, max=most).astype(held_as)


def setup_inputs(seed: int = 0) -> dict:
    streams_of = jax.random.split(jax.random.key(seed), 5)
    return {
        "tensor3": normal_values(streams_of[0], (RI, NU, NU), 1.0, 6.0, ((0, 4), (1, 8))),
        "pattern": place_ends((jax.random.randint(streams_of[1], (RI // BLK, NU // BLK, NU // BLK), 0, 3) < 2).astype(jnp.int32), jax.random.fold_in(streams_of[1], 1), 0, 1),
        "orbitals": normal_values(streams_of[2], (NU, OCC), (NU * 256) ** -0.5, 0.015625, ((0, 8),)),
        "metric": draw_metric(jax.random.fold_in(streams_of[4], 71), 0),
    }


def contract_block(inputs):
    tensor_block, block_mask = inputs
    cell_mask = jnp.repeat(jnp.repeat(block_mask, BLK, axis=0), BLK, axis=1).astype(jnp.bfloat16)
    masked = tensor_block * cell_mask[None]
    product = jnp.dot(masked.reshape(BLK * NU, NU), orbitals_global[0], preferred_element_type=jnp.float32)
    return product.astype(jnp.bfloat16).reshape(BLK, NU, OCC)


orbitals_global = []


def reference(tensor3, pattern, orbitals, metric):
    def contract_one(inputs):
        tensor_block, block_mask = inputs
        cell_mask = jnp.repeat(jnp.repeat(block_mask, BLK, axis=0), BLK, axis=1).astype(jnp.bfloat16)
        masked = tensor_block * cell_mask[None]
        product = jnp.dot(masked.reshape(BLK * NU, NU), orbitals, preferred_element_type=jnp.float32)
        return product.astype(jnp.bfloat16).reshape(BLK, NU, OCC)

    blocks = tensor3.reshape(RI // BLK, BLK, NU, NU)
    coeffs = lax.map(contract_one, (blocks, pattern)).reshape(RI, NU, OCC)
    fitted = jnp.dot(metric, coeffs.reshape(RI, NU * OCC), preferred_element_type=jnp.float32)
    fitted = fitted.astype(jnp.bfloat16).reshape(RI, NU, OCC)

    def accumulate(running, row_pair):
        fit_row, coef_row = row_pair
        return running - jnp.dot(fit_row, coef_row.T, preferred_element_type=jnp.float32), None

    exchange_matrix, unused = lax.scan(accumulate, jnp.zeros((NU, NU), jnp.float32), (fitted, coeffs))
    return exchange_matrix
```

```python
import functools

import jax
import jax.numpy as jnp
from jax import lax
from jax.experimental import pallas as pl
from jax.experimental.pallas import tpu as pltpu
from jax.sharding import PartitionSpec as P

MESH = pl.DeviceIdType.MESH


def kernel(nw, nn, t_ref, ct_ref, metric_ref, k_ref, wide_c, send, recv, gram, send_sem, recv_sem):
    ndev = nw * nn
    ri_local, ao_local, _ = t_ref.shape
    occ = ct_ref.shape[0]
    half = ri_local // 2
    lanes = 2 * ao_local
    chunks = occ // (2 * ndev)
    my_w, my_n = lax.axis_index("wide"), lax.axis_index("narrow")
    me = my_w * nn + my_n

    barrier = pltpu.get_barrier_semaphore()

    def greet(step, carry):
        other = lax.rem(me + step, ndev)
        pl.semaphore_signal(
            barrier, inc=1, device_id=(other // nn, lax.rem(other, nn)), device_id_type=MESH
        )
        return carry

    lax.fori_loop(1, ndev, greet, 0)

    def contract(step, carry):
        r = step * 2
        rows = jnp.concatenate(
            [t_ref[r], t_ref[half + r], t_ref[r + 1], t_ref[half + r + 1]], axis=0
        )
        out = lax.dot_general(
            ct_ref[...], rows, (((1,), (1,)), ((), ())), preferred_element_type=jnp.float32
        )
        start = pl.multiple_of(r * occ, 2 * occ)
        wide_c[pl.ds(start, occ), :] = out[:, :lanes]
        wide_c[pl.ds(start + occ, occ), :] = out[:, lanes:]
        return carry

    lax.fori_loop(0, half // 2, contract, 0)

    low = lax.broadcasted_iota(jnp.int32, (half, lanes), 1) < ao_local
    rows_here = pl.ds(pl.multiple_of(my_w * ri_local, ri_local), ri_local)
    lanes_here = pl.ds(pl.multiple_of(my_n * lanes, lanes), lanes)

    def pack(chunk, other):
        first = wide_c[pl.ds(chunk * 2 * ndev + other, half, stride=occ), :]
        second = wide_c[pl.ds(chunk * 2 * ndev + ndev + other, half, stride=occ), :]
        top = jnp.where(low, first, pltpu.roll(second, ao_local, 1))
        bottom = jnp.where(low, pltpu.roll(first, ao_local, 1), second)
        send[chunk, other] = jnp.concatenate([top, bottom], axis=0).astype(jnp.bfloat16)

    def outgoing(chunk, other):
        return pltpu.make_async_remote_copy(
            src_ref=send.at[chunk, other],
            dst_ref=recv.at[chunk, rows_here, lanes_here],
            send_sem=send_sem.at[chunk],
            recv_sem=recv_sem.at[chunk],
            device_id=(other // nn, lax.rem(other, nn)),
            device_id_type=MESH,
        )

    def own(chunk):
        return pltpu.make_async_copy(
            send.at[chunk, me], recv.at[chunk, rows_here, lanes_here], recv_sem.at[chunk]
        )

    pl.semaphore_wait(barrier, ndev - 1)
    for chunk in range(chunks):
        def ship(step, carry, chunk=chunk):
            other = lax.rem(me + step, ndev)
            pack(chunk, other)
            outgoing(chunk, other).start()
            return carry

        lax.fori_loop(1, ndev, ship, 0)
        pack(chunk, me)
        own(chunk).start()

    width = 2 * lanes
    for chunk in range(chunks):
        pltpu.make_async_copy(recv.at[chunk], recv.at[chunk], recv_sem.at[chunk]).wait()

        def fit(step, carry, chunk=chunk):
            at = pl.ds(pl.multiple_of(step * width, width), width)
            fitted = jnp.dot(
                metric_ref[...], recv[chunk, :, at], preferred_element_type=jnp.float32
            ).astype(jnp.bfloat16)
            term = lax.dot_general(
                fitted, recv[chunk], (((0,), (0,)), ((), ())), preferred_element_type=jnp.float32
            )
            gram[at, :] = term if chunk == 0 else gram[at, :] + term
            return carry

        lax.fori_loop(0, nn // 2, fit, 0)

    left = lax.broadcasted_iota(jnp.int32, (ao_local, lanes), 1) < ao_local

    def fold(n, carry):
        even = pl.ds(pl.multiple_of(n * lanes, lanes), ao_local)
        odd = pl.ds(pl.multiple_of(n * lanes + ao_local, ao_local), ao_local)
        out = pl.ds(pl.multiple_of(n * ao_local, ao_local), ao_local)
        for pair in range(nn // 2):
            one, two = pl.ds(2 * pair * lanes, lanes), pl.ds((2 * pair + 1) * lanes, lanes)
            here = jnp.where(left, gram[even, one], gram[odd, two])
            there = jnp.where(left, gram[even, two], gram[odd, one])
            k_ref[out, pl.ds(pair * lanes, lanes)] = -(here + pltpu.roll(there, ao_local, 1))
        return carry

    lax.fori_loop(0, nn, fold, 0)

    for chunk in range(chunks):
        def sent(step, carry, chunk=chunk):
            outgoing(chunk, lax.rem(me + step, ndev)).wait_send()
            return carry

        lax.fori_loop(1, ndev, sent, 0)


def body(nw, nn, tensor3, pattern, orbitals, metric):
    ri_local, ao_local, basis = tensor3.shape
    occ = orbitals.shape[1]
    ndev = nw * nn
    chunks = occ // (2 * ndev)
    lanes = 2 * ao_local
    block = basis // pattern.shape[2]
    keep = jnp.repeat(pattern[0, 0], block).astype(jnp.bfloat16)
    ct = (lax.all_gather(orbitals, "narrow", axis=0, tiled=True) * keep[:, None]).T
    term = pl.pallas_call(
        functools.partial(kernel, nw, nn),
        out_shape=jax.ShapeDtypeStruct((basis, basis), jnp.float32),
        in_specs=[pl.BlockSpec(memory_space=pltpu.VMEM)] * 3,
        out_specs=pl.BlockSpec(memory_space=pltpu.VMEM),
        scratch_shapes=[
            pltpu.VMEM((ri_local // 2 * occ, lanes), jnp.float32),
            pltpu.VMEM((chunks, ndev, ri_local, lanes), jnp.bfloat16),
            pltpu.VMEM((chunks, nw * ri_local, nn * lanes), jnp.bfloat16),
            pltpu.VMEM((nn * lanes, nn * lanes), jnp.float32),
            pltpu.SemaphoreType.DMA((chunks,)),
            pltpu.SemaphoreType.DMA((chunks,)),
        ],
        compiler_params=pltpu.CompilerParams(
            collective_id=0, has_side_effects=True, vmem_limit_bytes=56 * 1024 * 1024
        ),
    )(tensor3, ct, metric)
    return lax.psum_scatter(term, ("wide", "narrow"), scatter_dimension=0, tiled=True)


def solution(mesh):
    nw, nn = mesh.shape["wide"], mesh.shape["narrow"]
    in_specs = (P("wide", "narrow", None), P("wide", "narrow", None), P("narrow", None), P())
    out_specs = P(("wide", "narrow"), None)
    return jax.shard_map(
        functools.partial(body, nw, nn), mesh=mesh, in_specs=in_specs, out_specs=out_specs, check_vma=False
    )
```

```python
import functools

import jax
import jax.numpy as jnp
from jax import lax
from jax.experimental import pallas as pl
from jax.experimental.pallas import tpu as pltpu
from jax.sharding import PartitionSpec as P

MESH = pl.DeviceIdType.MESH


def kernel(nw, nn, pattern_ref, t_hbm, orb_ref, metric_ref, out_ref, t_ref, orbs, ct_ref, wide_c, send, recv, gram,
           terms, from_core, from_wide, from_z, t_sem, orb_send, orb_recv, send_sem, recv_sem,
           core_send, core_recv, wide_send, wide_recv, z_send, z_recv):
    ndev = nw * nn
    ri_local, ao_local, _ = t_ref.shape
    occ = ct_ref.shape[0]
    half = ri_local // 2
    lanes = 2 * ao_local
    chunks = occ // (2 * ndev)
    zs = nn // 2
    my_w, my_n = lax.axis_index("wide"), lax.axis_index("narrow")
    me = my_w * nn + my_n
    my_z, my_core = my_n // 2, lax.rem(my_n, 2)

    t_copy = pltpu.make_async_copy(t_hbm, t_ref, t_sem)
    t_copy.start()
    barrier = pltpu.get_barrier_semaphore()

    def greet(step, carry):
        other = lax.rem(me + step, ndev)
        pl.semaphore_signal(
            barrier, inc=1, device_id=(other // nn, lax.rem(other, nn)), device_id_type=MESH
        )
        return carry

    lax.fori_loop(1, ndev, greet, 0)
    pl.semaphore_wait(barrier, ndev - 1)

    def orbital_copy(other, source):
        return pltpu.make_async_remote_copy(
            src_ref=orb_ref,
            dst_ref=orbs.at[source],
            send_sem=orb_send.at[other],
            recv_sem=orb_recv.at[source],
            device_id=(my_w, other),
            device_id_type=MESH,
        )

    for step in range(1, nn):
        orbital_copy(lax.rem(my_n + step, nn), my_n).start()
    orbs[my_n] = orb_ref[...]
    for step in range(1, nn):
        other = lax.rem(my_n + step, nn)
        orbital_copy(other, other).wait_recv()
    for pair in range(nn // 2):
        kept = [
            orbs[n].astype(jnp.float32) * pattern_ref[0, 0, n].astype(jnp.float32)
            for n in (2 * pair, 2 * pair + 1)
        ]
        ct_ref[:, pair * lanes:(pair + 1) * lanes] = jnp.concatenate(kept, axis=0).T.astype(jnp.bfloat16)
    t_copy.wait()

    def contract(step, carry):
        r = step * 2
        rows = jnp.concatenate(
            [t_ref[r], t_ref[half + r], t_ref[r + 1], t_ref[half + r + 1]], axis=0
        )
        out = lax.dot_general(
            ct_ref[...], rows, (((1,), (1,)), ((), ())), preferred_element_type=jnp.float32
        )
        start = pl.multiple_of(r * occ, 2 * occ)
        wide_c[pl.ds(start, occ), :] = out[:, :lanes]
        wide_c[pl.ds(start + occ, occ), :] = out[:, lanes:]
        return carry

    lax.fori_loop(0, half // 2, contract, 0)

    low = lax.broadcasted_iota(jnp.int32, (half, lanes), 1) < ao_local
    rows_here = pl.ds(pl.multiple_of(my_w * ri_local, ri_local), ri_local)
    lanes_here = pl.ds(pl.multiple_of(my_n * lanes, lanes), lanes)

    def pack(chunk, other):
        first = wide_c[pl.ds(chunk * 2 * ndev + other, half, stride=occ), :]
        second = wide_c[pl.ds(chunk * 2 * ndev + ndev + other, half, stride=occ), :]
        top = jnp.where(low, first, pltpu.roll(second, ao_local, 1))
        bottom = jnp.where(low, pltpu.roll(first, ao_local, 1), second)
        send[chunk, other] = jnp.concatenate([top, bottom], axis=0).astype(jnp.bfloat16)

    def outgoing(chunk, other):
        return pltpu.make_async_remote_copy(
            src_ref=send.at[chunk, other],
            dst_ref=recv.at[chunk, rows_here, lanes_here],
            send_sem=send_sem.at[chunk],
            recv_sem=recv_sem.at[chunk],
            device_id=(other // nn, lax.rem(other, nn)),
            device_id_type=MESH,
        )

    def own(chunk):
        return pltpu.make_async_copy(
            send.at[chunk, me], recv.at[chunk, rows_here, lanes_here], recv_sem.at[chunk]
        )

    for chunk in range(chunks):
        def ship(step, carry, chunk=chunk):
            other = lax.rem(me + step, ndev)
            pack(chunk, other)
            outgoing(chunk, other).start()
            return carry

        lax.fori_loop(1, ndev, ship, 0)
        pack(chunk, me)
        own(chunk).start()

    width = 2 * lanes
    for chunk in range(chunks):
        pltpu.make_async_copy(recv.at[chunk], recv.at[chunk], recv_sem.at[chunk]).wait()

        def fit(step, carry, chunk=chunk):
            at = pl.ds(pl.multiple_of(step * width, width), width)
            fitted = jnp.dot(
                metric_ref[...], recv[chunk, :, at], preferred_element_type=jnp.float32
            ).astype(jnp.bfloat16)
            term = lax.dot_general(
                fitted, recv[chunk], (((0,), (0,)), ((), ())), preferred_element_type=jnp.float32
            )
            gram[at, :] = term if chunk == 0 else gram[at, :] + term
            return carry

        lax.fori_loop(0, nn // 2, fit, 0)

    left = lax.broadcasted_iota(jnp.int32, (ao_local, lanes), 1) < ao_local
    rows = ao_local // nw

    def fold(n, carry):
        even = pl.ds(pl.multiple_of(n * lanes, lanes), ao_local)
        odd = pl.ds(pl.multiple_of(n * lanes + ao_local, ao_local), ao_local)
        for pair in range(nn // 2):
            one, two = pl.ds(2 * pair * lanes, lanes), pl.ds((2 * pair + 1) * lanes, lanes)
            here = jnp.where(left, gram[even, one], gram[odd, two])
            there = jnp.where(left, gram[even, two], gram[odd, one])
            folded = -(here + pltpu.roll(there, ao_local, 1))
            for q in range(nw):
                block = n * nw + q
                terms[q % 2, block // nn, lax.rem(block, nn) // 2, :, pl.ds(pair * lanes, lanes)] = (
                    folded[q * rows:(q + 1) * rows]
                )
        return carry

    lax.fori_loop(0, nn, fold, 0)

    def to_core(w):
        return pltpu.make_async_remote_copy(
            src_ref=terms.at[1 - my_core, w],
            dst_ref=from_core.at[w],
            send_sem=core_send.at[w],
            recv_sem=core_recv.at[w],
            device_id=(my_w, my_z * 2 + 1 - my_core),
            device_id_type=MESH,
        )

    def to_wide(other, source):
        return pltpu.make_async_remote_copy(
            src_ref=terms.at[my_core, other],
            dst_ref=from_wide.at[source],
            send_sem=wide_send.at[other],
            recv_sem=wide_recv.at[source],
            device_id=(other, my_n),
            device_id_type=MESH,
        )

    def to_z(other, source):
        return pltpu.make_async_remote_copy(
            src_ref=terms.at[my_core, my_w, other],
            dst_ref=from_z.at[source],
            send_sem=z_send.at[other],
            recv_sem=z_recv.at[source],
            device_id=(my_w, other * 2 + my_core),
            device_id_type=MESH,
        )

    wides = [lax.rem(my_w + step, nw) for step in range(1, nw)]
    levels = [lax.rem(my_z + step, zs) for step in range(1, zs)]
    for w in wides + [my_w]:
        to_core(w).start()
    for w in wides + [my_w]:
        to_core(w).wait_recv()
        terms[my_core, w] = terms[my_core, w] + from_core[w]
        if w is not my_w:
            to_wide(w, my_w).start()
    for w in wides:
        to_wide(w, w).wait_recv()
    for z in levels + [my_z]:
        total = terms[my_core, my_w, z]
        for w in wides:
            total = total + from_wide[w, z]
        terms[my_core, my_w, z] = total
        if z is not my_z:
            to_z(z, my_z).start()
    total = terms[my_core, my_w, my_z]
    for z in levels:
        to_z(z, z).wait_recv()
        total = total + from_z[z]
    out_ref[...] = total

    for step in range(1, nn):
        orbital_copy(lax.rem(my_n + step, nn), my_n).wait_send()
    for w in wides + [my_w]:
        to_core(w).wait_send()
    for w in wides:
        to_wide(w, my_w).wait_send()
    for z in levels:
        to_z(z, my_z).wait_send()
    for chunk in range(chunks):
        def sent(step, carry, chunk=chunk):
            outgoing(chunk, lax.rem(me + step, ndev)).wait_send()
            return carry

        lax.fori_loop(1, ndev, sent, 0)


def body(nw, nn, tensor3, pattern, orbitals, metric):
    ri_local, ao_local, basis = tensor3.shape
    occ = orbitals.shape[1]
    ndev = nw * nn
    chunks = occ // (2 * ndev)
    lanes = 2 * ao_local
    rows = ao_local // nw
    assert pattern.shape == (1, 1, nn) and basis == nn * ao_local and occ == chunks * 2 * ndev
    vmem = pl.BlockSpec(memory_space=pltpu.VMEM)
    return pl.pallas_call(
        functools.partial(kernel, nw, nn),
        out_shape=jax.ShapeDtypeStruct((rows, basis), jnp.float32),
        in_specs=[pl.BlockSpec(memory_space=pltpu.SMEM), pl.BlockSpec(memory_space=pl.ANY), vmem, vmem],
        out_specs=vmem,
        scratch_shapes=[
            pltpu.VMEM(tensor3.shape, jnp.bfloat16),
            pltpu.VMEM((nn, ao_local, occ), jnp.bfloat16),
            pltpu.VMEM((occ, basis), jnp.bfloat16),
            pltpu.VMEM((ri_local // 2 * occ, lanes), jnp.float32),
            pltpu.VMEM((chunks, ndev, ri_local, lanes), jnp.bfloat16),
            pltpu.VMEM((chunks, nw * ri_local, nn * lanes), jnp.bfloat16),
            pltpu.VMEM((nn * lanes, nn * lanes), jnp.float32),
            pltpu.VMEM((2, nw, nn // 2, rows, basis), jnp.float32),
            pltpu.VMEM((nw, nn // 2, rows, basis), jnp.float32),
            pltpu.VMEM((nw, nn // 2, rows, basis), jnp.float32),
            pltpu.VMEM((nn // 2, rows, basis), jnp.float32),
            pltpu.SemaphoreType.DMA,
            pltpu.SemaphoreType.DMA((nn,)),
            pltpu.SemaphoreType.DMA((nn,)),
            pltpu.SemaphoreType.DMA((chunks,)),
            pltpu.SemaphoreType.DMA((chunks,)),
            pltpu.SemaphoreType.DMA((nw,)),
            pltpu.SemaphoreType.DMA((nw,)),
            pltpu.SemaphoreType.DMA((nw,)),
            pltpu.SemaphoreType.DMA((nw,)),
            pltpu.SemaphoreType.DMA((nn // 2,)),
            pltpu.SemaphoreType.DMA((nn // 2,)),
        ],
        compiler_params=pltpu.CompilerParams(
            collective_id=0, has_side_effects=True, vmem_limit_bytes=56 * 1024 * 1024
        ),
    )(pattern, tensor3, orbitals, metric)


def solution(mesh):
    nw, nn = mesh.shape["wide"], mesh.shape["narrow"]
    in_specs = (P("wide", "narrow", None), P("wide", "narrow", None), P("narrow", None), P())
    out_specs = P(("wide", "narrow"), None)
    return jax.shard_map(
        functools.partial(body, nw, nn), mesh=mesh, in_specs=in_specs, out_specs=out_specs, check_vma=False
    )
```

```python
import functools

import jax
import jax.numpy as jnp
from jax import lax
from jax.experimental import pallas as pl
from jax.experimental.pallas import tpu as pltpu
from jax.sharding import PartitionSpec as P

MESH = pl.DeviceIdType.MESH


def kernel(nw, nn, pattern_ref, t_hbm, orb_ref, metric_ref, out_ref, t_ref, orbs, ct_ref, wide_c, send, recv, gram,
           terms, from_core, from_wide, from_z, t_sem, orb_send, orb_recv, pass_send, send_sem, recv_sem,
           core_send, core_recv, wide_send, wide_recv, z_send, z_recv):
    ndev = nw * nn
    ri_local, ao_local, _ = t_ref.shape
    occ = ct_ref.shape[0]
    part = ri_local // 4
    lanes = 2 * ao_local
    chunks = occ // (2 * ndev)
    zs = nn // 2
    my_w, my_n = lax.axis_index("wide"), lax.axis_index("narrow")
    me = my_w * nn + my_n
    my_z, my_core = my_n // 2, lax.rem(my_n, 2)

    t_copy = pltpu.make_async_copy(t_hbm, t_ref, t_sem)
    t_copy.start()
    barrier = pltpu.get_barrier_semaphore()

    def greet(step, carry):
        other = lax.rem(me + step, ndev)
        pl.semaphore_signal(
            barrier, inc=1, device_id=(other // nn, lax.rem(other, nn)), device_id_type=MESH
        )
        return carry

    lax.fori_loop(1, ndev, greet, 0)
    pl.semaphore_wait(barrier, ndev - 1)

    levels = [lax.rem(my_z + step, zs) for step in range(1, zs)]

    def orbital_copy(z, core, source):
        return pltpu.make_async_remote_copy(
            src_ref=orb_ref,
            dst_ref=orbs.at[source],
            send_sem=orb_send.at[z * 2 + core],
            recv_sem=orb_recv.at[source],
            device_id=(my_w, z * 2 + core),
            device_id_type=MESH,
        )

    def forward(z):
        return pltpu.make_async_remote_copy(
            src_ref=orbs.at[z * 2 + my_core],
            dst_ref=orbs.at[z * 2 + my_core],
            send_sem=pass_send.at[z],
            recv_sem=orb_recv.at[z * 2 + my_core],
            device_id=(my_w, my_z * 2 + 1 - my_core),
            device_id_type=MESH,
        )

    def landed(source):
        pltpu.make_async_remote_copy(
            src_ref=orb_ref, dst_ref=orbs.at[source], send_sem=orb_send.at[source],
            recv_sem=orb_recv.at[source], device_id=(my_w, source), device_id_type=MESH,
        ).wait_recv()

    for z in levels:
        orbital_copy(z, my_core, my_n).start()
    orbital_copy(my_z, 1 - my_core, my_n).start()
    orbs[my_n] = orb_ref[...]
    for z in levels:
        landed(z * 2 + my_core)
        forward(z).start()
    for z in [my_z] + levels:
        landed(z * 2 + 1 - my_core)
        kept = [
            orbs[n].astype(jnp.float32) * pattern_ref[0, 0, n].astype(jnp.float32)
            for n in (2 * z, 2 * z + 1)
        ]
        at = pl.ds(pl.multiple_of(z * lanes, lanes), lanes)
        ct_ref[:, at] = jnp.concatenate(kept, axis=0).T.astype(jnp.bfloat16)
    t_copy.wait()

    def contract(step, carry):
        r = step * 2
        first = r // part * 2 * part + lax.rem(r, part)
        rows = jnp.concatenate(
            [t_ref[first], t_ref[first + part], t_ref[first + 1], t_ref[first + part + 1]], axis=0
        )
        out = lax.dot_general(
            ct_ref[...], rows, (((1,), (1,)), ((), ())), preferred_element_type=jnp.float32
        )
        start = pl.multiple_of(r * occ, 2 * occ)
        wide_c[pl.ds(start, occ), :] = out[:, :lanes]
        wide_c[pl.ds(start + occ, occ), :] = out[:, lanes:]
        return carry

    low = lax.broadcasted_iota(jnp.int32, (part, lanes), 1) < ao_local
    lanes_here = pl.ds(pl.multiple_of(my_n * lanes, lanes), lanes)

    def pack(chunk, other, group):
        at = group * part * occ + chunk * 2 * ndev + other
        first = wide_c[pl.ds(at, part, stride=occ), :]
        second = wide_c[pl.ds(at + ndev, part, stride=occ), :]
        top = jnp.where(low, first, pltpu.roll(second, ao_local, 1))
        bottom = jnp.where(low, pltpu.roll(first, ao_local, 1), second)
        send[chunk, other, pl.ds(group * 2 * part, 2 * part)] = jnp.concatenate(
            [top, bottom], axis=0
        ).astype(jnp.bfloat16)

    def rows_here(start, count):
        return pl.ds(pl.multiple_of(my_w * ri_local + start, count), count)

    def outgoing(chunk, other, start, count):
        return pltpu.make_async_remote_copy(
            src_ref=send.at[chunk, other, pl.ds(start, count)],
            dst_ref=recv.at[chunk, rows_here(start, count), lanes_here],
            send_sem=send_sem.at[chunk],
            recv_sem=recv_sem.at[chunk],
            device_id=(other // nn, lax.rem(other, nn)),
            device_id_type=MESH,
        )

    def to_all(act):
        far = [zs // 2] + [x for x in range(1, zs) if x != zs // 2] + [0]
        for x in far:
            def one(step, carry, x=x):
                w = lax.rem(my_w + step // 2, nw)
                core = lax.rem(my_core + step, 2)
                act(w * nn + lax.rem(my_z + x, zs) * 2 + core)
                return carry

            lax.fori_loop(0 if x else 1, 2 * nw, one, 0)

    for group in range(2):
        lax.fori_loop(group * part // 2, (group + 1) * part // 2, contract, 0)

        def ship_part(other, group=group):
            pack(0, other, group)
            outgoing(0, other, group * 2 * part, 2 * part).start()

        to_all(ship_part)
        pack(0, me, group)
    for chunk in range(1, chunks):
        def ship(other, chunk=chunk):
            pack(chunk, other, 0)
            pack(chunk, other, 1)
            outgoing(chunk, other, 0, ri_local).start()

        to_all(ship)
        pack(chunk, me, 0)
        pack(chunk, me, 1)
    for chunk in range(chunks):
        pltpu.make_async_copy(
            send.at[chunk, me], recv.at[chunk, rows_here(0, ri_local), lanes_here], recv_sem.at[chunk]
        ).start()

    per = nn // nw
    width = per * lanes

    def arrived(chunk):
        pltpu.make_async_copy(recv.at[chunk], recv.at[chunk], recv_sem.at[chunk]).wait()

    def fit(chunk, w):
        at = pl.ds(pl.multiple_of(w * width, width), width)
        fitted = jnp.dot(
            metric_ref[...], recv[chunk, :, at], preferred_element_type=jnp.float32
        ).astype(jnp.bfloat16)
        term = lax.dot_general(
            fitted, recv[chunk], (((0,), (0,)), ((), ())), preferred_element_type=jnp.float32
        )
        gram[at, :] = term if chunk == 0 else gram[at, :] + term

    for chunk in range(chunks - 1):
        arrived(chunk)

        def fit_one(w, carry, chunk=chunk):
            fit(chunk, w)
            return carry

        lax.fori_loop(0, nw, fit_one, 0)

    left = lax.broadcasted_iota(jnp.int32, (ao_local, lanes), 1) < ao_local
    rows = ao_local // nw

    def fold(w):
        for n in range(per):
            start = w * width + n * lanes
            even = pl.ds(pl.multiple_of(start, lanes), ao_local)
            odd = pl.ds(pl.multiple_of(start + ao_local, ao_local), ao_local)
            for pair in range(nn // 2):
                one, two = pl.ds(2 * pair * lanes, lanes), pl.ds((2 * pair + 1) * lanes, lanes)
                here = jnp.where(left, gram[even, one], gram[odd, two])
                there = jnp.where(left, gram[even, two], gram[odd, one])
                folded = -(here + pltpu.roll(there, ao_local, 1))
                for q in range(nw):
                    terms[q % 2, w, (n * nw + q) // 2, :, pl.ds(pair * lanes, lanes)] = (
                        folded[q * rows:(q + 1) * rows]
                    )

    def to_core(w):
        return pltpu.make_async_remote_copy(
            src_ref=terms.at[1 - my_core, w],
            dst_ref=from_core.at[w],
            send_sem=core_send.at[w],
            recv_sem=core_recv.at[w],
            device_id=(my_w, my_z * 2 + 1 - my_core),
            device_id_type=MESH,
        )

    def to_wide(other, source):
        return pltpu.make_async_remote_copy(
            src_ref=terms.at[my_core, other],
            dst_ref=from_wide.at[source],
            send_sem=wide_send.at[other],
            recv_sem=wide_recv.at[source],
            device_id=(other, my_n),
            device_id_type=MESH,
        )

    def to_z(other, source):
        return pltpu.make_async_remote_copy(
            src_ref=terms.at[my_core, my_w, other],
            dst_ref=from_z.at[source],
            send_sem=z_send.at[other],
            recv_sem=z_recv.at[source],
            device_id=(my_w, other * 2 + my_core),
            device_id_type=MESH,
        )

    wides = [lax.rem(my_w + step, nw) for step in range(1, nw)]
    def pass_on(w):
        to_core(w).wait_recv()
        terms[my_core, w] = terms[my_core, w] + from_core[w]
        if w is not my_w:
            to_wide(w, my_w).start()

    arrived(chunks - 1)
    before = None
    for w in wides + [my_w]:
        fit(chunks - 1, w)
        fold(w)
        to_core(w).start()
        if before is not None:
            pass_on(before)
        before = w
    pass_on(before)
    for w in wides:
        to_wide(w, w).wait_recv()
    for z in levels + [my_z]:
        total = terms[my_core, my_w, z]
        for w in wides:
            total = total + from_wide[w, z]
        terms[my_core, my_w, z] = total
        if z is not my_z:
            to_z(z, my_z).start()
    total = terms[my_core, my_w, my_z]
    for z in levels:
        to_z(z, z).wait_recv()
        total = total + from_z[z]
    out_ref[...] = total

    for z in levels:
        orbital_copy(z, my_core, my_n).wait_send()
        forward(z).wait_send()
    orbital_copy(my_z, 1 - my_core, my_n).wait_send()
    for w in wides + [my_w]:
        to_core(w).wait_send()
    for w in wides:
        to_wide(w, my_w).wait_send()
    for z in levels:
        to_z(z, my_z).wait_send()
    for chunk in range(chunks):
        def sent(other, chunk=chunk):
            outgoing(chunk, other, 0, ri_local).wait_send()

        to_all(sent)


def body(nw, nn, tensor3, pattern, orbitals, metric):
    ri_local, ao_local, basis = tensor3.shape
    occ = orbitals.shape[1]
    ndev = nw * nn
    chunks = occ // (2 * ndev)
    lanes = 2 * ao_local
    rows = ao_local // nw
    assert pattern.shape == (1, 1, nn) and basis == nn * ao_local and occ == chunks * 2 * ndev
    vmem = pl.BlockSpec(memory_space=pltpu.VMEM)
    return pl.pallas_call(
        functools.partial(kernel, nw, nn),
        out_shape=jax.ShapeDtypeStruct((rows, basis), jnp.float32),
        in_specs=[pl.BlockSpec(memory_space=pltpu.SMEM), pl.BlockSpec(memory_space=pl.ANY), vmem, vmem],
        out_specs=vmem,
        scratch_shapes=[
            pltpu.VMEM(tensor3.shape, jnp.bfloat16),
            pltpu.VMEM((nn, ao_local, occ), jnp.bfloat16),
            pltpu.VMEM((occ, basis), jnp.bfloat16),
            pltpu.VMEM((ri_local // 2 * occ, lanes), jnp.float32),
            pltpu.VMEM((chunks, ndev, ri_local, lanes), jnp.bfloat16),
            pltpu.VMEM((chunks, nw * ri_local, nn * lanes), jnp.bfloat16),
            pltpu.VMEM((nn * lanes, nn * lanes), jnp.float32),
            pltpu.VMEM((2, nw, nn // 2, rows, basis), jnp.float32),
            pltpu.VMEM((nw, nn // 2, rows, basis), jnp.float32),
            pltpu.VMEM((nw, nn // 2, rows, basis), jnp.float32),
            pltpu.VMEM((nn // 2, rows, basis), jnp.float32),
            pltpu.SemaphoreType.DMA,
            pltpu.SemaphoreType.DMA((nn,)),
            pltpu.SemaphoreType.DMA((nn,)),
            pltpu.SemaphoreType.DMA((nn // 2,)),
            pltpu.SemaphoreType.DMA((chunks,)),
            pltpu.SemaphoreType.DMA((chunks,)),
            pltpu.SemaphoreType.DMA((nw,)),
            pltpu.SemaphoreType.DMA((nw,)),
            pltpu.SemaphoreType.DMA((nw,)),
            pltpu.SemaphoreType.DMA((nw,)),
            pltpu.SemaphoreType.DMA((nn // 2,)),
            pltpu.SemaphoreType.DMA((nn // 2,)),
        ],
        compiler_params=pltpu.CompilerParams(
            collective_id=0, has_side_effects=True, vmem_limit_bytes=56 * 1024 * 1024
        ),
    )(pattern, tensor3, orbitals, metric)


def solution(mesh):
    nw, nn = mesh.shape["wide"], mesh.shape["narrow"]
    in_specs = (P("wide", "narrow", None), P("wide", "narrow", None), P("narrow", None), P())
    out_specs = P(("wide", "narrow"), None)
    return jax.shard_map(
        functools.partial(body, nw, nn), mesh=mesh, in_specs=in_specs, out_specs=out_specs, check_vma=False
    )
```
